256 devices in a mesh: tr: 32 (over y_hi, z, core), pt: 8 (over x, y_lo).
Axes of the slice: x: 4, y: 4 (y_hi: 2, y_lo: 2; y = y_hi * 2 + y_lo), z: 8, core: 2. Of those that a mesh axis runs over, the one named last changes fastest.
Arguments:
- gathers: bfloat16 [8192, 64, 1024], P(('tr', 'pt')), may hold values from -6 to 6
- level_one: bfloat16 [2048, 256, 256], P(('tr', 'pt')), may hold values from -0.375 to 0.375
- level_two: bfloat16 [8192, 64, 256], P(('tr', 'pt')), may hold values from -0.375 to 0.375
- middle: bfloat16 [8192, 64, 64], P(('tr', 'pt')), may hold values from -0.75 to 0.75
- level_three: bfloat16 [8192, 64, 256], P(('tr', 'pt')), may hold values from -0.375 to 0.375
Outputs:
- imaged: bfloat16 [8192, 64, 1024], P(('tr', 'pt'))
The draws below stay inside these ranges and needn't reach their ends.
All inputs are finite; a program needn't handle non-finite values.
Results may differ from the reference program's by a relative error of at most 0.0064.
Values may be sent and summed in bfloat16 or wider, within the bound.
No kernel may reach another device: no remote copies, remote signals or barrier semaphores. Data moves between devices by JAX's collectives and lax.ppermute only.
A program may use at most 128 MiB of HBM per device.

```python
import jax
import jax.numpy as jnp
from jax import lax

R = 64
BLK = 32
G = 1024
P_SIZE = 8192
N_TR = 32
N_PT = 8


def shard_levels(own_key, extent, cuts, smallest, largest):
    loudness = 1.0
    for axis_at, blocks in cuts:
        draws = jax.random.uniform(jax.random.fold_in(jax.random.fold_in(own_key, 6), axis_at), (blocks,), jnp.float32, smallest / len(cuts), largest / len(cuts))
        loudness = loudness * jnp.repeat(jnp.exp(draws), extent[axis_at] // blocks).reshape((-1,) + (1,) * (len(extent) - 1 - axis_at))
    return loudness


def bell_draw(stream_key, dims, scale, bound, pieces=(), held_as=jnp.bfloat16):
    result = scale * jax.random.normal(stream_key, dims, jnp.float32)
    if pieces:
        result = result * shard_levels(stream_key, dims, pieces, -0.22, 0.18)
    return jnp.clip(result, -bound, bound).astype(held_as)


def setup_inputs(seed: int = 0) -> dict:
    keys = jax.random.split(jax.random.key(seed), 6)
    gathers = bell_draw(keys[0], (P_SIZE, R, G), 1.0, 6.0, ((0, 256),))
    level_one = bell_draw(keys[1], (P_SIZE // 4, 4 * R, 4 * R), (4 * R) ** -0.5, 0.375, ((0, 256),))
    level_two = bell_draw(keys[2], (P_SIZE, R, 4 * R), (4 * R) ** -0.5, 0.375, ((0, 256),))
    middle = bell_draw(keys[3], (P_SIZE, R, R), R ** -0.5, 0.75, ((0, 256),))
    level_three = bell_draw(keys[4], (P_SIZE, R, 4 * R), (4 * R) ** -0.5, 0.375, ((0, 256),))
    return dict(gathers=gathers, level_one=level_one, level_two=level_two, middle=middle, level_three=level_three)


def first_level(slab, weights):
    grouped = slab.reshape(-1, 4 * R, G).astype(jnp.float32)
    mixed = jnp.einsum('qik,qkg->qig', weights.astype(jnp.float32), grouped)
    return mixed.astype(jnp.bfloat16).reshape(slab.shape)


def partner_level(slab, weights, top_bit):
    spread = slab.shape[0]
    half_blocks = BLK // 2
    if top_bit:
        parts = slab.reshape(2, spread // 2, 2, half_blocks, R, G).transpose(1, 0, 2, 3, 4, 5)
        rows = weights.reshape(2, spread // 2, 2, half_blocks, R, 4 * R).transpose(1, 0, 2, 3, 4, 5)
    else:
        parts = slab.reshape(spread // 2, 2, 2, half_blocks, R, G)
        rows = weights.reshape(spread // 2, 2, 2, half_blocks, R, 4 * R)
    inputs = parts.transpose(0, 3, 1, 2, 4, 5).reshape(spread // 2, half_blocks, 4 * R, G)
    mixed = jnp.einsum('lahjrk,ljkg->lahjrg', rows.astype(jnp.float32), inputs.astype(jnp.float32))
    mixed = mixed.astype(jnp.bfloat16)
    if top_bit:
        mixed = mixed.transpose(1, 0, 2, 3, 4, 5)
    return mixed.reshape(spread, BLK, R, G)


def section_before(operands):
    slab, weights_one, weights_two = operands
    first = first_level(slab, weights_one)
    return partner_level(first.reshape(N_PT, BLK, R, G), weights_two, True)


def section_after(operands):
    slab, centre, weights_three = operands
    centred = jnp.einsum('sbrk,sbkg->sbrg', centre.astype(jnp.float32), slab.astype(jnp.float32))
    return partner_level(centred.astype(jnp.bfloat16), weights_three, False)


def reference(gathers, level_one, level_two, middle, level_three):
    spans = BLK // N_TR
    second = lax.map(section_before, (gathers.reshape(N_TR, N_PT * BLK, R, G),
                                    level_one.reshape(N_TR, N_PT * BLK // 4, 4 * R, 4 * R),
                                    level_two.reshape(N_TR, N_PT, BLK, R, 4 * R)))
    moved = second.reshape(N_TR, N_PT, N_TR, spans, R, G).transpose(2, 1, 0, 3, 4, 5)
    moved = moved.reshape(N_TR, N_PT, BLK, R, G)
    imaged = lax.map(section_after, (moved, middle.reshape(N_TR, N_PT, BLK, R, R),
                                   level_three.reshape(N_TR, N_PT, BLK, R, 4 * R)))
    return imaged.reshape(N_TR * N_PT * BLK, R, G)
```

```python
import functools

import jax
import jax.numpy as jnp
from jax import lax
from jax.experimental import pallas as pl
from jax.experimental.pallas import tpu as pltpu
from jax.sharding import PartitionSpec as P

AXES = ("tr", "pt")
CHUNKS = ((0, 128), (256, 256), (512, 256), (768, 256), (128, 128))
STEPS = 4
VMEM = 32 * 1024 * 1024


def exchanged(array, flip_tr, flip_pt):
    n_tr, n_pt = lax.axis_size("tr"), lax.axis_size("pt")
    pairs = [
        (t * n_pt + s, (t ^ flip_tr) * n_pt + (s ^ flip_pt))
        for t in range(n_tr)
        for s in range(n_pt)
    ]
    return lax.ppermute(array, AXES, pairs)


def spread(array):
    n = lax.axis_size("tr") // 2
    groups = [[h * n + i for i in range(n)] for h in range(2)]
    return lax.all_to_all(
        array, "tr", split_axis=0, concat_axis=0, tiled=True, axis_index_groups=groups
    )


def params():
    return pltpu.CompilerParams(vmem_limit_bytes=VMEM)


def cost(flops, moved):
    return pl.CostEstimate(flops=flops, bytes_accessed=moved, transcendentals=0)


def level_one_kernel(weights, values, out):
    for q in range(weights.shape[0]):
        rows = values[4 * q : 4 * q + 4].reshape(weights.shape[2], values.shape[2])
        product = jnp.dot(weights[q], rows, preferred_element_type=jnp.float32)
        out[4 * q : 4 * q + 4] = product.astype(out.dtype).reshape(4, *out.shape[1:])


def level_one_chunk(weights, values, start, size):
    blocks, rank, _ = values.shape
    groups = weights.shape[0]
    column = start // size
    return pl.pallas_call(
        level_one_kernel,
        grid=(STEPS,),
        in_specs=[
            pl.BlockSpec((groups // STEPS, 4 * rank, 4 * rank), lambda i: (i, 0, 0)),
            pl.BlockSpec((blocks // STEPS, rank, size), lambda i: (i, 0, column)),
        ],
        out_specs=pl.BlockSpec((blocks // STEPS, rank, size), lambda i: (i, 0, 0)),
        out_shape=jax.ShapeDtypeStruct((blocks, rank, size), jnp.bfloat16),
        compiler_params=params(),
        cost_estimate=cost(2 * blocks * rank * 4 * rank * size, 4 * blocks * rank * size),
    )(weights, values)


def order_kernel(flags, weights, out):
    groups = out.shape[0]
    rank = weights.shape[1]
    upper_s, upper_t = flags[0], flags[1]
    for j in range(groups):
        for row in range(2):
            half = upper_t if row == 0 else 1 - upper_t
            block = weights[j + groups * half]
            low, high = block[:, : 2 * rank], block[:, 2 * rank :]
            rows = slice(row * rank, (row + 1) * rank)
            out[j, rows, : 2 * rank] = jnp.where(upper_s == 1, high, low)
            out[j, rows, 2 * rank :] = jnp.where(upper_s == 1, low, high)


def ordered_two(flags, weights):
    blocks, rank, depth = weights.shape
    return pl.pallas_call(
        order_kernel,
        in_specs=[
            pl.BlockSpec(memory_space=pltpu.SMEM),
            pl.BlockSpec(memory_space=pltpu.VMEM),
        ],
        out_specs=pl.BlockSpec(memory_space=pltpu.VMEM),
        out_shape=jax.ShapeDtypeStruct((blocks // 2, 2 * rank, depth), jnp.bfloat16),
        compiler_params=params(),
        cost_estimate=cost(0, 4 * blocks * rank * depth),
    )(flags, weights)


def level_two_kernel(weights, own, other, kept, sent):
    rank, size = own.shape[2:]
    for j in range(own.shape[1]):
        rows = jnp.concatenate([own[0, j], own[1, j], other[0, j], other[1, j]], axis=0)
        product = jnp.dot(weights[j], rows, preferred_element_type=jnp.float32)
        product = product.astype(kept.dtype)
        kept[j] = product[:rank]
        sent[j] = product[rank:]


def level_two_chunk(weights, own, other):
    blocks, rank, size = own.shape
    half = blocks // 2
    part = half // STEPS
    pair = pl.BlockSpec((2, part, rank, size), lambda i: (0, i, 0, 0))
    out = jax.ShapeDtypeStruct((half, rank, size), jnp.bfloat16)
    out_spec = pl.BlockSpec((part, rank, size), lambda i: (i, 0, 0))
    return pl.pallas_call(
        level_two_kernel,
        grid=(STEPS,),
        in_specs=[
            pl.BlockSpec((part, 2 * rank, 4 * rank), lambda i: (i, 0, 0)),
            pair,
            pair,
        ],
        out_specs=[out_spec, out_spec],
        out_shape=[out, out],
        compiler_params=params(),
        cost_estimate=cost(2 * blocks * rank * 4 * rank * size, 6 * blocks * rank * size),
    )(weights, own.reshape(2, half, rank, size), other.reshape(2, half, rank, size))


def compose_kernel(flags, weights, middle, partner, out):
    groups, rank = out.shape[0], weights.shape[1]

    def for_place(low_s, upper_t):
        for j in range(groups):
            rows = jnp.concatenate([weights[j], weights[j + groups]], axis=0)
            for slot in range(4):
                e, f = low_s ^ (slot & 1), upper_t ^ (slot >> 1)
                centre = (partner if slot & 1 else middle)[j + groups * f]
                at = (2 * e + f) * rank
                product = jnp.dot(
                    rows[:, at : at + rank], centre, preferred_element_type=jnp.float32
                )
                out[j, :, slot * rank : (slot + 1) * rank] = product.astype(out.dtype)

    for low_s in range(2):
        for upper_t in range(2):
            here = (flags[2] == low_s) & (flags[1] == upper_t)
            pl.when(here)(functools.partial(for_place, low_s, upper_t))


def composed_three(flags, weights, middle, partner):
    blocks, rank, depth = weights.shape
    return pl.pallas_call(
        compose_kernel,
        in_specs=[pl.BlockSpec(memory_space=pltpu.SMEM)]
        + [pl.BlockSpec(memory_space=pltpu.VMEM)] * 3,
        out_specs=pl.BlockSpec(memory_space=pltpu.VMEM),
        out_shape=jax.ShapeDtypeStruct((blocks // 2, 2 * rank, depth), jnp.bfloat16),
        compiler_params=params(),
        cost_estimate=cost(2 * blocks * rank * depth * rank, 6 * blocks * rank * depth),
    )(flags, weights, middle, partner)


def level_three_kernel(weights, *refs):
    pieces, out = refs[:4], refs[-1]
    rank = out.shape[2]
    for j in range(out.shape[1]):
        rows = jnp.concatenate([piece[j] for piece in pieces], axis=0)
        product = jnp.dot(weights[j], rows, preferred_element_type=jnp.float32)
        product = product.astype(out.dtype)
        out[0, j] = product[:rank]
        out[1, j] = product[rank:]


def level_three_chunk(weights, pieces, result, shape, start):
    half, rank, size = pieces[0].shape
    part = half // STEPS
    column = start // size
    in_specs = [pl.BlockSpec((part, 2 * rank, 4 * rank), lambda i: (i, 0, 0))]
    in_specs += [pl.BlockSpec((part, rank, size), lambda i: (i, 0, 0))] * 4
    operands, aliases = [weights, *pieces], {}
    if result is not None:
        in_specs.append(pl.BlockSpec(memory_space=pl.ANY))
        operands.append(result)
        aliases = {5: 0}
    return pl.pallas_call(
        level_three_kernel,
        grid=(STEPS,),
        in_specs=in_specs,
        out_specs=pl.BlockSpec((2, part, rank, size), lambda i: (0, i, 0, column)),
        out_shape=jax.ShapeDtypeStruct((2, half, rank, shape[2]), jnp.bfloat16),
        input_output_aliases=aliases,
        compiler_params=params(),
        cost_estimate=cost(4 * half * rank * 4 * rank * size, 12 * half * rank * size),
    )(*operands)


def shards(gathers, level_one, level_two, middle, level_three):
    n_tr, n_pt = lax.axis_size("tr"), lax.axis_size("pt")
    t, s = lax.axis_index("tr"), lax.axis_index("pt")
    flags = jnp.stack([s // (n_pt // 2), t // (n_tr // 2), s % 2]).astype(jnp.int32)
    partner = exchanged(middle, 0, 1)
    weights_two = ordered_two(flags, level_two)
    weights_three = composed_three(flags, level_three, middle, partner)
    result = None
    for start, size in CHUNKS:
        own = level_one_chunk(level_one, gathers, start, size)
        other = exchanged(own, 0, n_pt // 2)
        kept, sent = level_two_chunk(weights_two, own, other)
        kept, sent = spread(kept), spread(sent)
        pieces = (
            kept,
            exchanged(kept, 0, 1),
            exchanged(sent, n_tr // 2, 0),
            exchanged(sent, n_tr // 2, 1),
        )
        result = level_three_chunk(weights_three, pieces, result, gathers.shape, start)
    return result.reshape(gathers.shape)


def solution(mesh):
    spec = P(("tr", "pt"), None, None)
    return jax.shard_map(
        shards, mesh=mesh, in_specs=(spec,) * 5, out_specs=spec, check_vma=False
    )
```

```python
import functools

import jax
import jax.numpy as jnp
from jax import lax
from jax.experimental import pallas as pl
from jax.experimental.pallas import tpu as pltpu
from jax.sharding import PartitionSpec as P

AXES = ("tr", "pt")
CHUNKS = ((0, 128), (256, 256), (512, 256), (768, 256), (128, 128))
STEPS = 4
VMEM = 24 * 1024 * 1024


def exchanged(array, flip_tr, flip_pt):
    n_tr, n_pt = lax.axis_size("tr"), lax.axis_size("pt")
    pairs = [
        (t * n_pt + s, (t ^ flip_tr) * n_pt + (s ^ flip_pt))
        for t in range(n_tr)
        for s in range(n_pt)
    ]
    return lax.ppermute(array, AXES, pairs)


def spread(array):
    n = lax.axis_size("tr") // 2
    groups = [[h * n + i for i in range(n)] for h in range(2)]
    return lax.all_to_all(
        array, "tr", split_axis=0, concat_axis=0, tiled=True, axis_index_groups=groups
    )


def params():
    return pltpu.CompilerParams(vmem_limit_bytes=VMEM)


def cost(flops, moved):
    return pl.CostEstimate(flops=100000000000, bytes_accessed=370000000, transcendentals=0)


def ordered_call(kernel, operands, in_specs, after=(), aliases=None, **kwargs):
    n = len(operands)
    after = [x for x in after if not any(x is y for y in operands)]

    def body(*refs):
        kernel(*refs[:n], *refs[n + len(after) :])

    specs = list(in_specs) + [pl.BlockSpec(memory_space=pltpu.HBM)] * len(after)
    return pl.pallas_call(
        body,
        in_specs=specs,
        input_output_aliases=aliases or {},
        compiler_params=params(),
        **kwargs,
    )(*operands, *after)


def level_one_kernel(chunks, weights, values, *refs):
    outs, (weight_buf, buf, sems) = refs[: len(chunks)], refs[len(chunks) :]
    groups = weights.shape[0]
    part, start, width = groups // STEPS, chunks[0][2], buf.shape[2]
    copies = []
    for i in range(STEPS):
        for k, (source, target, n) in enumerate(
            ((weights, weight_buf, part), (values.at[:, :, start : start + width], buf, 4 * part))
        ):
            rows = pl.ds(i * n, n)
            copy = pltpu.make_async_copy(source.at[rows], target.at[rows], sems.at[i, k])
            copy.start()
            copies.append(copy)
    for i in range(STEPS):
        copies[2 * i].wait()
        copies[2 * i + 1].wait()
        for q in range(i * part, (i + 1) * part):
            rows = buf[4 * q : 4 * q + 4].reshape(weights.shape[2], width)
            product = jnp.dot(weight_buf[q], rows, preferred_element_type=jnp.float32)
            product = product.astype(jnp.bfloat16).reshape(4, -1, width)
            for (at, size, _), out in zip(chunks, outs):
                out[4 * q : 4 * q + 4] = product[:, :, at - start : at - start + size]


def level_one_chunks(weights, values, chunks, after):
    blocks, rank, _ = values.shape
    start = min(at for at, _ in chunks)
    width = max(at + size for at, size in chunks) - start
    chunks = tuple((at, size, start) for at, size in chunks)
    return ordered_call(
        functools.partial(level_one_kernel, chunks),
        [weights, values],
        [pl.BlockSpec(memory_space=pltpu.HBM)] * 2,
        after,
        out_specs=[pl.BlockSpec(memory_space=pltpu.VMEM)] * len(chunks),
        out_shape=[
            jax.ShapeDtypeStruct((blocks, rank, size), jnp.bfloat16) for _, size, _ in chunks
        ],
        scratch_shapes=[
            pltpu.VMEM(weights.shape, jnp.bfloat16),
            pltpu.VMEM((blocks, rank, width), jnp.bfloat16),
            pltpu.SemaphoreType.DMA((STEPS, 2)),
        ],
        cost_estimate=cost(0, 0),
        name="one",
    )


def order_kernel(flags, weights, out):
    groups = out.shape[0]
    rank = weights.shape[1]
    upper_s, upper_t = flags[0], flags[1]
    for j in range(groups):
        for row in range(2):
            half = upper_t if row == 0 else 1 - upper_t
            block = weights[j + groups * half]
            low, high = block[:, : 2 * rank], block[:, 2 * rank :]
            rows = slice(row * rank, (row + 1) * rank)
            out[j, rows, : 2 * rank] = jnp.where(upper_s == 1, high, low)
            out[j, rows, 2 * rank :] = jnp.where(upper_s == 1, low, high)


def ordered_two(flags, weights, after):
    blocks, rank, depth = weights.shape
    return ordered_call(
        order_kernel,
        [flags, weights],
        [
            pl.BlockSpec(memory_space=pltpu.SMEM),
            pl.BlockSpec(memory_space=pltpu.VMEM),
        ],
        after,
        out_specs=pl.BlockSpec(memory_space=pltpu.VMEM),
        out_shape=jax.ShapeDtypeStruct((blocks // 2, 2 * rank, depth), jnp.bfloat16),
        cost_estimate=cost(0, 4 * blocks * rank * depth),
        name="order",
    )


def level_two_kernel(weights, own, other, out):
    rank, size = own.shape[2:]
    for j in range(own.shape[1]):
        rows = jnp.concatenate([own[0, j], own[1, j], other[0, j], other[1, j]], axis=0)
        product = jnp.dot(weights[j], rows, preferred_element_type=jnp.float32)
        out[j] = product.astype(out.dtype).reshape(2, rank, size)


def level_two_chunk(weights, own, other, after):
    blocks, rank, size = own.shape
    half = blocks // 2
    part = half // STEPS
    pair = pl.BlockSpec((2, part, rank, size), lambda i: (0, i, 0, 0))
    return ordered_call(
        level_two_kernel,
        [weights, own.reshape(2, half, rank, size), other.reshape(2, half, rank, size)],
        [pl.BlockSpec((part, 2 * rank, 4 * rank), lambda i: (i, 0, 0)), pair, pair],
        after,
        grid=(STEPS,),
        out_specs=pl.BlockSpec((part, 2, rank, size), lambda i: (i, 0, 0, 0)),
        out_shape=jax.ShapeDtypeStruct((half, 2, rank, size), jnp.bfloat16),
        cost_estimate=pl.CostEstimate(flops=100000000000, bytes_accessed=370000000, transcendentals=0),
        name="two",
    )


def split_kernel(both, kept, sent):
    kept[...] = both[:, 0]
    sent[...] = both[:, 1]


def split_chunk(both, after):
    half, _, rank, size = both.shape
    part = half // 2
    out = jax.ShapeDtypeStruct((half, rank, size), jnp.bfloat16)
    out_spec = pl.BlockSpec((part, rank, size), lambda i: (i, 0, 0))
    return ordered_call(
        split_kernel,
        [both],
        [pl.BlockSpec((part, 2, rank, size), lambda i: (i, 0, 0, 0))],
        after,
        grid=(2,),
        out_specs=[out_spec, out_spec],
        out_shape=[out, out],
        cost_estimate=cost(0, 8 * half * rank * size),
        name="split",
    )


def compose_kernel(flags, weights, middle, partner, out):
    groups, rank = out.shape[0], weights.shape[1]

    def for_place(low_s, upper_t):
        for j in range(groups):
            rows = jnp.concatenate([weights[j], weights[j + groups]], axis=0)
            for slot in range(4):
                e, f = low_s ^ (slot & 1), upper_t ^ (slot >> 1)
                centre = (partner if slot & 1 else middle)[j + groups * f]
                at = (2 * e + f) * rank
                product = jnp.dot(
                    rows[:, at : at + rank], centre, preferred_element_type=jnp.float32
                )
                out[j, :, slot * rank : (slot + 1) * rank] = product.astype(out.dtype)

    for low_s in range(2):
        for upper_t in range(2):
            here = (flags[2] == low_s) & (flags[1] == upper_t)
            pl.when(here)(functools.partial(for_place, low_s, upper_t))


def composed_three(flags, weights, middle, partner, after):
    blocks, rank, depth = weights.shape
    return ordered_call(
        compose_kernel,
        [flags, weights, middle, partner],
        [pl.BlockSpec(memory_space=pltpu.SMEM)]
        + [pl.BlockSpec(memory_space=pltpu.VMEM)] * 3,
        after,
        out_specs=pl.BlockSpec(memory_space=pltpu.VMEM),
        out_shape=jax.ShapeDtypeStruct((blocks // 2, 2 * rank, depth), jnp.bfloat16),
        cost_estimate=cost(2 * blocks * rank * depth * rank, 6 * blocks * rank * depth),
        name="compose",
    )


def level_three_kernel(weights, *refs):
    pieces, out = refs[:4], refs[-1]
    rank = out.shape[2]
    for j in range(out.shape[1]):
        rows = jnp.concatenate([piece[j] for piece in pieces], axis=0)
        product = jnp.dot(weights[j], rows, preferred_element_type=jnp.float32)
        product = product.astype(out.dtype)
        out[0, j] = product[:rank]
        out[1, j] = product[rank:]


def level_three_chunk(weights, pieces, result, shape, start, after):
    half, rank, size = pieces[0].shape
    part = half // STEPS
    column = start // size
    in_specs = [pl.BlockSpec((part, 2 * rank, 4 * rank), lambda i: (i, 0, 0))]
    in_specs += [pl.BlockSpec((part, rank, size), lambda i: (i, 0, 0))] * 4
    operands, aliases = [weights, *pieces], {}
    if result is not None:
        in_specs.append(pl.BlockSpec(memory_space=pltpu.HBM))
        operands.append(result)
        aliases = {5: 0}
    return ordered_call(
        level_three_kernel,
        operands,
        in_specs,
        after,
        aliases,
        grid=(STEPS,),
        out_specs=pl.BlockSpec((2, part, rank, size), lambda i: (0, i, 0, column)),
        out_shape=jax.ShapeDtypeStruct((2, half, rank, shape[2]), jnp.bfloat16),
        cost_estimate=cost(4 * half * rank * 4 * rank * size, 12 * half * rank * size),
        name="three",
    )


def shards(gathers, level_one, level_two, middle, level_three):
    n_tr, n_pt = lax.axis_size("tr"), lax.axis_size("pt")
    t, s = lax.axis_index("tr"), lax.axis_index("pt")
    flags = jnp.stack([s >> 2, t >> 4, s & 1]).astype(jnp.int32)
    count = len(CHUNKS)
    own, other, both, pieces = {}, {}, {}, {}
    result, last = None, ()

    def one(cs):
        nonlocal last
        outs = level_one_chunks(level_one, gathers, [CHUNKS[c] for c in cs], last)
        last = (outs[0],)
        for c, out in zip(cs, outs):
            own[c] = out
            other[c] = exchanged(out, 0, n_pt // 2)

    def two(c):
        nonlocal last
        if c >= count:
            return
        mixed = level_two_chunk(weights_two, own[c], other[c], last)
        last = (mixed,)
        both[c] = spread(mixed)

    def split(c):
        nonlocal last
        kept, sent = split_chunk(both[c], last)
        last = (sent,)
        pieces[c] = (
            kept,
            exchanged(kept, 0, 1),
            exchanged(sent, n_tr // 2, 0),
            exchanged(sent, n_tr // 2, 1),
        )

    def three(c):
        nonlocal result, last
        if c < 0:
            return
        result = level_three_chunk(
            weights_three, pieces[c], result, gathers.shape, CHUNKS[c][0], last
        )
        last = (result,)

    partner = exchanged(middle, 0, 1)
    one([0])
    one(range(1, count))
    weights_two = ordered_two(flags, level_two, last)
    last = (weights_two,)
    two(0)
    weights_three = composed_three(flags, level_three, middle, partner, last)
    last = (weights_three,)
    two(1)
    for c in range(count):
        split(c)
        three(c - 1)
        two(c + 2)
    three(count - 1)
    return result.reshape(gathers.shape)


def solution(mesh):
    spec = P(("tr", "pt"), None, None)
    return jax.shard_map(
        shards, mesh=mesh, in_specs=(spec,) * 5, out_specs=spec, check_vma=False
    )
```

```python
import functools

import jax
import jax.numpy as jnp
from jax import lax
from jax.experimental import pallas as pl
from jax.experimental.pallas import tpu as pltpu
from jax.sharding import PartitionSpec as P

AXES = ("tr", "pt")
CHUNKS = ((0, 128), (256, 256), (512, 256), (768, 256), (128, 128))
STEPS = 4
VMEM = 24 * 1024 * 1024
WHOLE_VMEM = 60 * 1024 * 1024


def exchanged(array, flip_tr, flip_pt):
    n_tr, n_pt = lax.axis_size("tr"), lax.axis_size("pt")
    pairs = [
        (t * n_pt + s, (t ^ flip_tr) * n_pt + (s ^ flip_pt))
        for t in range(n_tr)
        for s in range(n_pt)
    ]
    return lax.ppermute(array, AXES, pairs)


def spread(array):
    n = lax.axis_size("tr") // 2
    groups = [[h * n + i for i in range(n)] for h in range(2)]
    return lax.all_to_all(
        array, "tr", split_axis=0, concat_axis=0, tiled=True, axis_index_groups=groups
    )


def params(vmem=VMEM):
    return pltpu.CompilerParams(vmem_limit_bytes=vmem)


def cost(flops, moved):
    return pl.CostEstimate(flops=100000000000, bytes_accessed=370000000, transcendentals=0)


def ordered_call(kernel, operands, in_specs, after=(), aliases=None, vmem=VMEM, **kwargs):
    n = len(operands)
    after = [x for x in after if not any(x is y for y in operands)]

    def body(*refs):
        kernel(*refs[:n], *refs[n + len(after) :])

    specs = list(in_specs) + [pl.BlockSpec(memory_space=pltpu.HBM)] * len(after)
    return pl.pallas_call(
        body,
        in_specs=specs,
        input_output_aliases=aliases or {},
        compiler_params=params(vmem),
        **kwargs,
    )(*operands, *after)


def level_one_kernel(chunks, weights, values, *refs):
    outs, (weight_buf, buf, sems) = refs[: len(chunks)], refs[len(chunks) :]
    groups = weights.shape[0]
    part, start, width = groups // STEPS, chunks[0][2], buf.shape[2]
    copies = []
    for i in range(STEPS):
        for k, (source, target, n) in enumerate(
            ((weights, weight_buf, part), (values.at[:, :, start : start + width], buf, 4 * part))
        ):
            rows = pl.ds(i * n, n)
            copy = pltpu.make_async_copy(source.at[rows], target.at[rows], sems.at[i, k])
            copy.start()
            copies.append(copy)
    for i in range(STEPS):
        copies[2 * i].wait()
        copies[2 * i + 1].wait()
        for q in range(i * part, (i + 1) * part):
            rows = buf[4 * q : 4 * q + 4].reshape(weights.shape[2], width)
            product = jnp.dot(weight_buf[q], rows, preferred_element_type=jnp.float32)
            product = product.astype(jnp.bfloat16).reshape(4, -1, width)
            for (at, size, _), out in zip(chunks, outs):
                out[4 * q : 4 * q + 4] = product[:, :, at - start : at - start + size]


def level_one_chunks(weights, values, chunks, after):
    blocks, rank, _ = values.shape
    start = min(at for at, _ in chunks)
    width = max(at + size for at, size in chunks) - start
    chunks = tuple((at, size, start) for at, size in chunks)
    return ordered_call(
        functools.partial(level_one_kernel, chunks),
        [weights, values],
        [pl.BlockSpec(memory_space=pltpu.HBM)] * 2,
        after,
        out_specs=[pl.BlockSpec(memory_space=pltpu.VMEM)] * len(chunks),
        out_shape=[
            jax.ShapeDtypeStruct((blocks, rank, size), jnp.bfloat16) for _, size, _ in chunks
        ],
        scratch_shapes=[
            pltpu.VMEM(weights.shape, jnp.bfloat16),
            pltpu.VMEM((blocks, rank, width), jnp.bfloat16),
            pltpu.SemaphoreType.DMA((STEPS, 2)),
        ],
        vmem=WHOLE_VMEM,
        cost_estimate=cost(0, 0),
        name="one",
    )


def order_kernel(flags, weights, out):
    groups = out.shape[0]
    rank = weights.shape[1]
    upper_s, upper_t = flags[0], flags[1]
    for j in range(groups):
        for row in range(2):
            half = upper_t if row == 0 else 1 - upper_t
            block = weights[j + groups * half]
            low, high = block[:, : 2 * rank], block[:, 2 * rank :]
            rows = slice(row * rank, (row + 1) * rank)
            out[j, rows, : 2 * rank] = jnp.where(upper_s == 1, high, low)
            out[j, rows, 2 * rank :] = jnp.where(upper_s == 1, low, high)


def ordered_two(flags, weights, after):
    blocks, rank, depth = weights.shape
    return ordered_call(
        order_kernel,
        [flags, weights],
        [
            pl.BlockSpec(memory_space=pltpu.SMEM),
            pl.BlockSpec(memory_space=pltpu.VMEM),
        ],
        after,
        out_specs=pl.BlockSpec(memory_space=pltpu.VMEM),
        out_shape=jax.ShapeDtypeStruct((blocks // 2, 2 * rank, depth), jnp.bfloat16),
        cost_estimate=cost(0, 4 * blocks * rank * depth),
        name="order",
    )


def level_two_kernel(weights, own, other, out):
    rank, size = own.shape[2:]
    for j in range(own.shape[1]):
        rows = jnp.concatenate([own[0, j], own[1, j], other[0, j], other[1, j]], axis=0)
        product = jnp.dot(weights[j], rows, preferred_element_type=jnp.float32)
        out[j] = product.astype(out.dtype).reshape(2, rank, size)


def level_two_chunk(weights, own, other, after):
    blocks, rank, size = own.shape
    half = blocks // 2
    part = half // 2
    pair = pl.BlockSpec((2, part, rank, size), lambda i: (0, i, 0, 0))
    return ordered_call(
        level_two_kernel,
        [weights, own.reshape(2, half, rank, size), other.reshape(2, half, rank, size)],
        [pl.BlockSpec((part, 2 * rank, 4 * rank), lambda i: (i, 0, 0)), pair, pair],
        after,
        grid=(2,),
        out_specs=pl.BlockSpec((part, 2, rank, size), lambda i: (i, 0, 0, 0)),
        out_shape=jax.ShapeDtypeStruct((half, 2, rank, size), jnp.bfloat16),
        cost_estimate=pl.CostEstimate(flops=100000000000, bytes_accessed=370000000, transcendentals=0),
        name="two",
    )


def level_two_apart_kernel(weights, own, other, kept, sent):
    rank = own.shape[2]
    for j in range(own.shape[1]):
        rows = jnp.concatenate([own[0, j], own[1, j], other[0, j], other[1, j]], axis=0)
        product = jnp.dot(weights[j], rows, preferred_element_type=jnp.float32)
        product = product.astype(kept.dtype)
        kept[j] = product[:rank]
        sent[j] = product[rank:]


def level_two_apart(weights, own, other, after):
    blocks, rank, size = own.shape
    half = blocks // 2
    part = half // 2
    pair = pl.BlockSpec((2, part, rank, size), lambda i: (0, i, 0, 0))
    return ordered_call(
        level_two_apart_kernel,
        [weights, own.reshape(2, half, rank, size), other.reshape(2, half, rank, size)],
        [pl.BlockSpec((part, 2 * rank, 4 * rank), lambda i: (i, 0, 0)), pair, pair],
        after,
        grid=(2,),
        out_specs=[pl.BlockSpec((part, rank, size), lambda i: (i, 0, 0))] * 2,
        out_shape=[jax.ShapeDtypeStruct((half, rank, size), jnp.bfloat16)] * 2,
        cost_estimate=cost(0, 0),
        name="apart",
    )


def pack_kernel(*refs):
    for i, ref in enumerate(refs[:4]):
        refs[4][:, i] = ref[...]


def pack_chunk(pieces, after):
    half, rank, size = pieces[0].shape
    part = half // 2
    return ordered_call(
        pack_kernel,
        pieces,
        [pl.BlockSpec((part, rank, size), lambda i: (i, 0, 0))] * 4,
        after,
        grid=(2,),
        out_specs=pl.BlockSpec((part, 4, rank, size), lambda i: (i, 0, 0, 0)),
        out_shape=jax.ShapeDtypeStruct((half, 4, rank, size), jnp.bfloat16),
        cost_estimate=cost(0, 0),
        name="pack",
    )


def split_kernel(both, kept, sent):
    kept[...] = both[:, 0]
    sent[...] = both[:, 1]


def split_chunk(both, after):
    half, _, rank, size = both.shape
    part = half // 2
    out = jax.ShapeDtypeStruct((half, rank, size), jnp.bfloat16)
    out_spec = pl.BlockSpec((part, rank, size), lambda i: (i, 0, 0))
    return ordered_call(
        split_kernel,
        [both],
        [pl.BlockSpec((part, 2, rank, size), lambda i: (i, 0, 0, 0))],
        after,
        grid=(2,),
        out_specs=[out_spec, out_spec],
        out_shape=[out, out],
        cost_estimate=cost(0, 8 * half * rank * size),
        name="split",
    )


def compose_kernel(flags, weights, middle, partner, out):
    groups, rank = out.shape[0], weights.shape[1]

    def for_place(low_s, upper_t):
        for j in range(groups):
            rows = jnp.concatenate([weights[j], weights[j + groups]], axis=0)
            for slot in range(4):
                e, f = low_s ^ (slot & 1), upper_t ^ (slot >> 1)
                centre = (partner if slot & 1 else middle)[j + groups * f]
                at = (2 * e + f) * rank
                product = jnp.dot(
                    rows[:, at : at + rank], centre, preferred_element_type=jnp.float32
                )
                out[j, :, slot * rank : (slot + 1) * rank] = product.astype(out.dtype)

    for low_s in range(2):
        for upper_t in range(2):
            here = (flags[2] == low_s) & (flags[1] == upper_t)
            pl.when(here)(functools.partial(for_place, low_s, upper_t))


def composed_three(flags, weights, middle, partner, after):
    blocks, rank, depth = weights.shape
    return ordered_call(
        compose_kernel,
        [flags, weights, middle, partner],
        [pl.BlockSpec(memory_space=pltpu.SMEM)]
        + [pl.BlockSpec(memory_space=pltpu.VMEM)] * 3,
        after,
        out_specs=pl.BlockSpec(memory_space=pltpu.VMEM),
        out_shape=jax.ShapeDtypeStruct((blocks // 2, 2 * rank, depth), jnp.bfloat16),
        cost_estimate=cost(2 * blocks * rank * depth * rank, 6 * blocks * rank * depth),
        name="compose",
    )


def level_three_kernel(count, weights, *refs):
    pieces, out, token = refs[:count], refs[-2], refs[-1]
    token[...] = jnp.zeros_like(token)
    rank = out.shape[2]
    for j in range(out.shape[1]):
        if len(pieces) == 1:
            rows = pieces[0][j].reshape(4 * rank, -1)
        else:
            rows = jnp.concatenate([piece[j] for piece in pieces], axis=0)
        product = jnp.dot(weights[j], rows, preferred_element_type=jnp.float32)
        product = product.astype(out.dtype)
        out[0, j] = product[:rank]
        out[1, j] = product[rank:]


def level_three_chunk(weights, pieces, result, shape, start, after):
    half, rank, size = pieces[0].shape[0], *pieces[0].shape[-2:]
    part = half // 2
    column = start // size
    in_specs = [pl.BlockSpec((part, 2 * rank, 4 * rank), lambda i: (i, 0, 0))]
    if len(pieces) == 1:
        in_specs.append(pl.BlockSpec((part, 4, rank, size), lambda i: (i, 0, 0, 0)))
    else:
        in_specs += [pl.BlockSpec((part, rank, size), lambda i: (i, 0, 0))] * 4
    operands, aliases = [weights, *pieces], {}
    if result is not None:
        in_specs.append(pl.BlockSpec(memory_space=pltpu.HBM))
        operands.append(result)
        aliases = {len(operands) - 1: 0}
    return ordered_call(
        functools.partial(level_three_kernel, len(pieces)),
        operands,
        in_specs,
        after,
        aliases,
        grid=(2,),
        out_specs=[
            pl.BlockSpec((2, part, rank, size), lambda i: (0, i, 0, column)),
            pl.BlockSpec((8, 128), lambda i: (0, 0)),
        ],
        out_shape=[
            jax.ShapeDtypeStruct((2, half, rank, shape[2]), jnp.bfloat16),
            jax.ShapeDtypeStruct((8, 128), jnp.float32),
        ],
        cost_estimate=cost(4 * half * rank * 4 * rank * size, 12 * half * rank * size),
        name="three",
    )


def shards(gathers, level_one, level_two, middle, level_three):
    n_tr, n_pt = lax.axis_size("tr"), lax.axis_size("pt")
    t, s = lax.axis_index("tr"), lax.axis_index("pt")
    flags = jnp.stack([s >> 2, t >> 4, s & 1]).astype(jnp.int32)
    count = len(CHUNKS)
    own, other, both, pieces = {}, {}, {}, {}
    result, last = None, ()

    def one(cs):
        nonlocal last
        outs = level_one_chunks(level_one, gathers, [CHUNKS[c] for c in cs], last)
        last = (outs[0],)
        for c, out in zip(cs, outs):
            own[c] = out
            other[c] = exchanged(out, 0, n_pt // 2)

    def two(c):
        nonlocal last
        if c >= count:
            return
        mixed = level_two_chunk(weights_two, own[c], other[c], last)
        last = (mixed,)
        both[c] = spread(mixed)

    def swapped(kept, sent):
        return (
            kept,
            exchanged(kept, 0, 1),
            exchanged(sent, n_tr // 2, 0),
            exchanged(sent, n_tr // 2, 1),
        )

    def apart(c):
        nonlocal last
        kept, sent = level_two_apart(weights_two, own[c], other[c], last)
        last = (sent,)
        pieces[c] = swapped(kept, sent)

    def pack(c):
        nonlocal last
        packed = pack_chunk(pieces[c], last)
        last = (packed,)
        pieces[c] = (spread(packed),)

    def split(c):
        nonlocal last
        kept, sent = split_chunk(both[c], last)
        last = (sent,)
        pieces[c] = swapped(kept, sent)

    def three(c):
        nonlocal result, last
        if c < 0:
            return
        result, token = level_three_chunk(
            weights_three, pieces[c], result, gathers.shape, CHUNKS[c][0], last
        )
        last = (token,)

    partner = exchanged(middle, 0, 1)
    one([0])
    one(range(1, count))
    weights_two = ordered_two(flags, level_two, last)
    last = (weights_two,)
    two(0)
    weights_three = composed_three(flags, level_three, middle, partner, last)
    last = (weights_three,)
    two(1)
    split(0)
    two(2)
    split(1)
    three(0)
    two(3)
    apart(4)
    split(2)
    three(1)
    pack(4)
    split(3)
    three(2)
    three(4)
    three(3)
    return result.reshape(gathers.shape)


def solution(mesh):
    spec = P(("tr", "pt"), None, None)
    return jax.shard_map(
        shards, mesh=mesh, in_specs=(spec,) * 5, out_specs=spec, check_vma=False
    )
```

```python
import functools

import jax
import jax.numpy as jnp
from jax import lax
from jax.experimental import pallas as pl
from jax.experimental.pallas import tpu as pltpu
from jax.sharding import PartitionSpec as P

AXES = ("tr", "pt")
CHUNKS = ((0, 128), (256, 256), (512, 256), (768, 256), (128, 128))
STEPS = 4
VMEM = 24 * 1024 * 1024
WHOLE_VMEM = 60 * 1024 * 1024


def exchanged(array, flip_tr, flip_pt):
    n_tr, n_pt = lax.axis_size("tr"), lax.axis_size("pt")
    pairs = [
        (t * n_pt + s, (t ^ flip_tr) * n_pt + (s ^ flip_pt))
        for t in range(n_tr)
        for s in range(n_pt)
    ]
    return lax.ppermute(array, AXES, pairs)


def spread(array):
    n = lax.axis_size("tr") // 2
    groups = [[h * n + i for i in range(n)] for h in range(2)]
    return lax.all_to_all(
        array, "tr", split_axis=0, concat_axis=0, tiled=True, axis_index_groups=groups
    )


def params(vmem=VMEM):
    return pltpu.CompilerParams(vmem_limit_bytes=vmem)


def cost(flops, moved):
    return pl.CostEstimate(flops=100000000000, bytes_accessed=370000000, transcendentals=0)


def ordered_call(kernel, operands, in_specs, after=(), aliases=None, vmem=VMEM, **kwargs):
    n = len(operands)
    after = [x for x in after if not any(x is y for y in operands)]

    def body(*refs):
        kernel(*refs[:n], *refs[n + len(after) :])

    specs = list(in_specs) + [pl.BlockSpec(memory_space=pltpu.HBM)] * len(after)
    return pl.pallas_call(
        body,
        in_specs=specs,
        input_output_aliases=aliases or {},
        compiler_params=params(vmem),
        **kwargs,
    )(*operands, *after)


def level_one_kernel(chunks, weights, values, *refs):
    outs, (weight_buf, buf, sems) = refs[: len(chunks)], refs[len(chunks) :]
    groups = weights.shape[0]
    part, start, width = groups // STEPS, chunks[0][2], buf.shape[2]
    copies = []
    for i in range(STEPS):
        for k, (source, target, n) in enumerate(
            ((weights, weight_buf, part), (values.at[:, :, start : start + width], buf, 4 * part))
        ):
            rows = pl.ds(i * n, n)
            copy = pltpu.make_async_copy(source.at[rows], target.at[rows], sems.at[i, k])
            copy.start()
            copies.append(copy)
    for i in range(STEPS):
        copies[2 * i].wait()
        copies[2 * i + 1].wait()
        for q in range(i * part, (i + 1) * part):
            rows = buf[4 * q : 4 * q + 4].reshape(weights.shape[2], width)
            product = jnp.dot(weight_buf[q], rows, preferred_element_type=jnp.float32)
            product = product.astype(jnp.bfloat16).reshape(4, -1, width)
            for (at, size, _), out in zip(chunks, outs):
                out[4 * q : 4 * q + 4] = product[:, :, at - start : at - start + size]


def level_one_chunks(weights, values, chunks, after):
    blocks, rank, _ = values.shape
    start = min(at for at, _ in chunks)
    width = max(at + size for at, size in chunks) - start
    chunks = tuple((at, size, start) for at, size in chunks)
    return ordered_call(
        functools.partial(level_one_kernel, chunks),
        [weights, values],
        [pl.BlockSpec(memory_space=pltpu.HBM)] * 2,
        after,
        out_specs=[pl.BlockSpec(memory_space=pltpu.VMEM)] * len(chunks),
        out_shape=[
            jax.ShapeDtypeStruct((blocks, rank, size), jnp.bfloat16) for _, size, _ in chunks
        ],
        scratch_shapes=[
            pltpu.VMEM(weights.shape, jnp.bfloat16),
            pltpu.VMEM((blocks, rank, width), jnp.bfloat16),
            pltpu.SemaphoreType.DMA((STEPS, 2)),
        ],
        vmem=WHOLE_VMEM,
        cost_estimate=cost(0, 0),
        name="one",
    )


def order_kernel(flags, weights, out):
    groups = out.shape[0]
    rank = weights.shape[1]
    upper_s, upper_t = flags[0], flags[1]
    for j in range(groups):
        for row in range(2):
            half = upper_t if row == 0 else 1 - upper_t
            block = weights[j + groups * half]
            low, high = block[:, : 2 * rank], block[:, 2 * rank :]
            rows = slice(row * rank, (row + 1) * rank)
            out[j, rows, : 2 * rank] = jnp.where(upper_s == 1, high, low)
            out[j, rows, 2 * rank :] = jnp.where(upper_s == 1, low, high)


def ordered_two(flags, weights, after):
    blocks, rank, depth = weights.shape
    return ordered_call(
        order_kernel,
        [flags, weights],
        [
            pl.BlockSpec(memory_space=pltpu.SMEM),
            pl.BlockSpec(memory_space=pltpu.VMEM),
        ],
        after,
        out_specs=pl.BlockSpec(memory_space=pltpu.VMEM),
        out_shape=jax.ShapeDtypeStruct((blocks // 2, 2 * rank, depth), jnp.bfloat16),
        cost_estimate=cost(0, 4 * blocks * rank * depth),
        name="order",
    )


def level_two_kernel(weights, own, other, out):
    rank, size = own.shape[2:]
    for j in range(own.shape[1]):
        rows = jnp.concatenate([own[0, j], own[1, j], other[0, j], other[1, j]], axis=0)
        product = jnp.dot(weights[j], rows, preferred_element_type=jnp.float32)
        out[j] = product.astype(out.dtype).reshape(2, rank, size)


def level_two_chunk(weights, own, other, after):
    blocks, rank, size = own.shape
    half = blocks // 2
    part = half // 2
    pair = pl.BlockSpec((2, part, rank, size), lambda i: (0, i, 0, 0))
    return ordered_call(
        level_two_kernel,
        [weights, own.reshape(2, half, rank, size), other.reshape(2, half, rank, size)],
        [pl.BlockSpec((part, 2 * rank, 4 * rank), lambda i: (i, 0, 0)), pair, pair],
        after,
        grid=(2,),
        out_specs=pl.BlockSpec((part, 2, rank, size), lambda i: (i, 0, 0, 0)),
        out_shape=jax.ShapeDtypeStruct((half, 2, rank, size), jnp.bfloat16),
        vmem=WHOLE_VMEM,
        cost_estimate=pl.CostEstimate(flops=100000000000, bytes_accessed=370000000, transcendentals=0),
        name="two",
    )


def level_two_apart_kernel(weights, own, other, kept, sent):
    rank = own.shape[2]
    for j in range(own.shape[1]):
        rows = jnp.concatenate([own[0, j], own[1, j], other[0, j], other[1, j]], axis=0)
        product = jnp.dot(weights[j], rows, preferred_element_type=jnp.float32)
        product = product.astype(kept.dtype)
        kept[j] = product[:rank]
        sent[j] = product[rank:]


def level_two_apart(weights, own, other, after):
    blocks, rank, size = own.shape
    half = blocks // 2
    part = half // 2
    pair = pl.BlockSpec((2, part, rank, size), lambda i: (0, i, 0, 0))
    return ordered_call(
        level_two_apart_kernel,
        [weights, own.reshape(2, half, rank, size), other.reshape(2, half, rank, size)],
        [pl.BlockSpec((part, 2 * rank, 4 * rank), lambda i: (i, 0, 0)), pair, pair],
        after,
        grid=(2,),
        out_specs=[pl.BlockSpec((part, rank, size), lambda i: (i, 0, 0))] * 2,
        out_shape=[jax.ShapeDtypeStruct((half, rank, size), jnp.bfloat16)] * 2,
        cost_estimate=cost(0, 0),
        name="apart",
    )


def pack_kernel(*refs):
    for i, ref in enumerate(refs[:4]):
        refs[4][:, i] = ref[...]


def pack_chunk(pieces, after):
    half, rank, size = pieces[0].shape
    part = half // 2
    return ordered_call(
        pack_kernel,
        pieces,
        [pl.BlockSpec((part, rank, size), lambda i: (i, 0, 0))] * 4,
        after,
        grid=(2,),
        out_specs=pl.BlockSpec((part, 4, rank, size), lambda i: (i, 0, 0, 0)),
        out_shape=jax.ShapeDtypeStruct((half, 4, rank, size), jnp.bfloat16),
        cost_estimate=cost(0, 0),
        name="pack",
    )


def split_kernel(both, kept, sent):
    kept[...] = both[:, 0]
    sent[...] = both[:, 1]


def split_chunk(both, after):
    half, _, rank, size = both.shape
    part = half // 2
    out = jax.ShapeDtypeStruct((half, rank, size), jnp.bfloat16)
    out_spec = pl.BlockSpec((part, rank, size), lambda i: (i, 0, 0))
    return ordered_call(
        split_kernel,
        [both],
        [pl.BlockSpec((part, 2, rank, size), lambda i: (i, 0, 0, 0))],
        after,
        grid=(2,),
        out_specs=[out_spec, out_spec],
        out_shape=[out, out],
        cost_estimate=cost(0, 8 * half * rank * size),
        name="split",
    )


def compose_kernel(flags, weights, middle, partner, out):
    groups, rank = out.shape[0], weights.shape[1]

    def for_place(low_s, upper_t):
        for j in range(groups):
            rows = jnp.concatenate([weights[j], weights[j + groups]], axis=0)
            for slot in range(4):
                e, f = low_s ^ (slot & 1), upper_t ^ (slot >> 1)
                centre = (partner if slot & 1 else middle)[j + groups * f]
                at = (2 * e + f) * rank
                product = jnp.dot(
                    rows[:, at : at + rank], centre, preferred_element_type=jnp.float32
                )
                out[j, :, slot * rank : (slot + 1) * rank] = product.astype(out.dtype)

    for low_s in range(2):
        for upper_t in range(2):
            here = (flags[2] == low_s) & (flags[1] == upper_t)
            pl.when(here)(functools.partial(for_place, low_s, upper_t))


def composed_three(flags, weights, middle, partner, after):
    blocks, rank, depth = weights.shape
    return ordered_call(
        compose_kernel,
        [flags, weights, middle, partner],
        [pl.BlockSpec(memory_space=pltpu.SMEM)]
        + [pl.BlockSpec(memory_space=pltpu.VMEM)] * 3,
        after,
        out_specs=pl.BlockSpec(memory_space=pltpu.VMEM),
        out_shape=jax.ShapeDtypeStruct((blocks // 2, 2 * rank, depth), jnp.bfloat16),
        cost_estimate=cost(2 * blocks * rank * depth * rank, 6 * blocks * rank * depth),
        name="compose",
    )


def level_three_kernel(count, weights, *refs):
    pieces, out, token = refs[:count], refs[-2], refs[-1]
    token[...] = jnp.zeros_like(token)
    rank = out.shape[2]
    for j in range(out.shape[1]):
        if len(pieces) == 1:
            rows = pieces[0][j].reshape(4 * rank, -1)
        else:
            rows = jnp.concatenate([piece[j] for piece in pieces], axis=0)
        product = jnp.dot(weights[j], rows, preferred_element_type=jnp.float32)
        product = product.astype(out.dtype)
        out[0, j] = product[:rank]
        out[1, j] = product[rank:]


def level_three_chunk(weights, pieces, result, shape, start, after):
    half, rank, size = pieces[0].shape[0], *pieces[0].shape[-2:]
    part = half // 2
    column = start // size
    in_specs = [pl.BlockSpec((part, 2 * rank, 4 * rank), lambda i: (i, 0, 0))]
    if len(pieces) == 1:
        in_specs.append(pl.BlockSpec((part, 4, rank, size), lambda i: (i, 0, 0, 0)))
    else:
        in_specs += [pl.BlockSpec((part, rank, size), lambda i: (i, 0, 0))] * 4
    operands, aliases = [weights, *pieces], {}
    if result is not None:
        in_specs.append(pl.BlockSpec(memory_space=pltpu.HBM))
        operands.append(result)
        aliases = {len(operands) - 1: 0}
    return ordered_call(
        functools.partial(level_three_kernel, len(pieces)),
        operands,
        in_specs,
        after,
        aliases,
        grid=(2,),
        out_specs=[
            pl.BlockSpec((2, part, rank, size), lambda i: (0, i, 0, column)),
            pl.BlockSpec((8, 128), lambda i: (0, 0)),
        ],
        out_shape=[
            jax.ShapeDtypeStruct((2, half, rank, shape[2]), jnp.bfloat16),
            jax.ShapeDtypeStruct((8, 128), jnp.float32),
        ],
        cost_estimate=cost(4 * half * rank * 4 * rank * size, 12 * half * rank * size),
        name="three",
    )


def shards(gathers, level_one, level_two, middle, level_three):
    n_tr, n_pt = lax.axis_size("tr"), lax.axis_size("pt")
    t, s = lax.axis_index("tr"), lax.axis_index("pt")
    flags = jnp.stack([s >> 2, t >> 4, s & 1]).astype(jnp.int32)
    count = len(CHUNKS)
    own, other, both, pieces = {}, {}, {}, {}
    result, last = None, ()

    def one(cs):
        nonlocal last
        outs = level_one_chunks(level_one, gathers, [CHUNKS[c] for c in cs], last)
        last = (outs[0],)
        for c, out in zip(cs, outs):
            own[c] = out
            other[c] = exchanged(out, 0, n_pt // 2)

    def two(c):
        nonlocal last
        if c >= count:
            return
        mixed = level_two_chunk(weights_two, own[c], other[c], last)
        last = (mixed,)
        both[c] = spread(mixed)

    def swapped(kept, sent):
        return (
            kept,
            exchanged(kept, 0, 1),
            exchanged(sent, n_tr // 2, 0),
            exchanged(sent, n_tr // 2, 1),
        )

    def apart(c):
        nonlocal last
        kept, sent = level_two_apart(weights_two, own[c], other[c], last)
        last = (sent,)
        pieces[c] = swapped(kept, sent)

    def pack(c):
        nonlocal last
        packed = pack_chunk(pieces[c], last)
        last = (packed,)
        pieces[c] = (spread(packed),)

    def split(c):
        nonlocal last
        kept, sent = split_chunk(both[c], last)
        last = (sent,)
        pieces[c] = swapped(kept, sent)

    def three(c):
        nonlocal result, last
        if c < 0:
            return
        result, token = level_three_chunk(
            weights_three, pieces[c], result, gathers.shape, CHUNKS[c][0], last
        )
        last = (token,)

    partner = exchanged(middle, 0, 1)
    one([0])
    one([1, 2, 3])
    weights_two = ordered_two(flags, level_two, last)
    last = (weights_two,)
    two(0)
    weights_three = composed_three(flags, level_three, middle, partner, last)
    last = (weights_three,)
    two(1)
    split(0)
    two(2)
    one([4])
    split(1)
    three(0)
    two(3)
    apart(4)
    split(2)
    three(1)
    pack(4)
    split(3)
    three(2)
    three(4)
    three(3)
    return result.reshape(gathers.shape)


def solution(mesh):
    spec = P(("tr", "pt"), None, None)
    return jax.shard_map(
        shards, mesh=mesh, in_specs=(spec,) * 5, out_specs=spec, check_vma=False
    )
```

```python
import functools

import jax
import jax.numpy as jnp
from jax import lax
from jax.experimental import pallas as pl
from jax.experimental.pallas import tpu as pltpu
from jax.sharding import PartitionSpec as P

AXES = ("tr", "pt")
CHUNKS = ((0, 128), (256, 256), (512, 256), (768, 256), (128, 128))
STEPS = 4
VMEM = 24 * 1024 * 1024
WHOLE_VMEM = 60 * 1024 * 1024


def exchanged(array, flip_tr, flip_pt):
    n_tr, n_pt = lax.axis_size("tr"), lax.axis_size("pt")
    pairs = [
        (t * n_pt + s, (t ^ flip_tr) * n_pt + (s ^ flip_pt))
        for t in range(n_tr)
        for s in range(n_pt)
    ]
    return lax.ppermute(array, AXES, pairs)


def spread(array):
    n = lax.axis_size("tr") // 2
    groups = [[h * n + i for i in range(n)] for h in range(2)]
    return lax.all_to_all(
        array, "tr", split_axis=0, concat_axis=0, tiled=True, axis_index_groups=groups
    )


def params(vmem=VMEM):
    return pltpu.CompilerParams(vmem_limit_bytes=vmem)


def cost(flops, moved):
    return pl.CostEstimate(flops=100000000000, bytes_accessed=370000000, transcendentals=0)


def ordered_call(kernel, operands, in_specs, after=(), aliases=None, vmem=VMEM, **kwargs):
    n = len(operands)
    after = [x for x in after if not any(x is y for y in operands)]

    def body(*refs):
        kernel(*refs[:n], *refs[n + len(after) :])

    specs = list(in_specs) + [pl.BlockSpec(memory_space=pltpu.HBM)] * len(after)
    return pl.pallas_call(
        body,
        in_specs=specs,
        input_output_aliases=aliases or {},
        compiler_params=params(vmem),
        **kwargs,
    )(*operands, *after)


def level_one_kernel(chunks, weights, values, *refs):
    outs, (weight_buf, buf, sems) = refs[: len(chunks)], refs[len(chunks) :]
    groups = weights.shape[0]
    part, start, width = groups // STEPS, chunks[0][2], buf.shape[2]
    copies = []
    for i in range(STEPS):
        for k, (source, target, n) in enumerate(
            ((weights, weight_buf, part), (values.at[:, :, start : start + width], buf, 4 * part))
        ):
            rows = pl.ds(i * n, n)
            copy = pltpu.make_async_copy(source.at[rows], target.at[rows], sems.at[i, k])
            copy.start()
            copies.append(copy)
    for i in range(STEPS):
        copies[2 * i].wait()
        copies[2 * i + 1].wait()
        for q in range(i * part, (i + 1) * part):
            rows = buf[4 * q : 4 * q + 4].reshape(weights.shape[2], width)
            product = jnp.dot(weight_buf[q], rows, preferred_element_type=jnp.float32)
            product = product.astype(jnp.bfloat16).reshape(4, -1, width)
            for (at, size, _), out in zip(chunks, outs):
                out[4 * q : 4 * q + 4] = product[:, :, at - start : at - start + size]


def level_one_chunks(weights, values, chunks, after):
    blocks, rank, _ = values.shape
    start = min(at for at, _ in chunks)
    width = max(at + size for at, size in chunks) - start
    chunks = tuple((at, size, start) for at, size in chunks)
    return ordered_call(
        functools.partial(level_one_kernel, chunks),
        [weights, values],
        [pl.BlockSpec(memory_space=pltpu.HBM)] * 2,
        after,
        out_specs=[pl.BlockSpec(memory_space=pltpu.VMEM)] * len(chunks),
        out_shape=[
            jax.ShapeDtypeStruct((blocks, rank, size), jnp.bfloat16) for _, size, _ in chunks
        ],
        scratch_shapes=[
            pltpu.VMEM(weights.shape, jnp.bfloat16),
            pltpu.VMEM((blocks, rank, width), jnp.bfloat16),
            pltpu.SemaphoreType.DMA((STEPS, 2)),
        ],
        vmem=WHOLE_VMEM,
        cost_estimate=cost(0, 0),
        name="one",
    )


def order_kernel(flags, weights, out):
    groups = out.shape[0]
    rank = weights.shape[1]
    upper_s, upper_t = flags[0], flags[1]
    for j in range(groups):
        for row in range(2):
            half = upper_t if row == 0 else 1 - upper_t
            block = weights[j + groups * half]
            low, high = block[:, : 2 * rank], block[:, 2 * rank :]
            rows = slice(row * rank, (row + 1) * rank)
            out[j, rows, : 2 * rank] = jnp.where(upper_s == 1, high, low)
            out[j, rows, 2 * rank :] = jnp.where(upper_s == 1, low, high)


def ordered_two(flags, weights, after):
    blocks, rank, depth = weights.shape
    return ordered_call(
        order_kernel,
        [flags, weights],
        [
            pl.BlockSpec(memory_space=pltpu.SMEM),
            pl.BlockSpec(memory_space=pltpu.VMEM),
        ],
        after,
        out_specs=pl.BlockSpec(memory_space=pltpu.VMEM),
        out_shape=jax.ShapeDtypeStruct((blocks // 2, 2 * rank, depth), jnp.bfloat16),
        cost_estimate=cost(0, 4 * blocks * rank * depth),
        name="order",
    )


def level_two_kernel(weights, own, other, out):
    rank, size = own.shape[2:]
    for j in range(own.shape[1]):
        rows = jnp.concatenate([own[0, j], own[1, j], other[0, j], other[1, j]], axis=0)
        product = jnp.dot(weights[j], rows, preferred_element_type=jnp.float32)
        out[j] = product.astype(out.dtype).reshape(2, rank, size)


def level_two_chunk(weights, own, other, after):
    blocks, rank, size = own.shape
    half = blocks // 2
    part = half // 2
    pair = pl.BlockSpec((2, part, rank, size), lambda i: (0, i, 0, 0))
    return ordered_call(
        level_two_kernel,
        [weights, own.reshape(2, half, rank, size), other.reshape(2, half, rank, size)],
        [pl.BlockSpec((part, 2 * rank, 4 * rank), lambda i: (i, 0, 0)), pair, pair],
        after,
        grid=(2,),
        out_specs=pl.BlockSpec((part, 2, rank, size), lambda i: (i, 0, 0, 0)),
        out_shape=jax.ShapeDtypeStruct((half, 2, rank, size), jnp.bfloat16),
        vmem=WHOLE_VMEM,
        cost_estimate=pl.CostEstimate(flops=100000000000, bytes_accessed=370000000, transcendentals=0),
        name="two",
    )


def level_two_apart_kernel(weights, own, other, kept, sent):
    rank = own.shape[2]
    for j in range(own.shape[1]):
        rows = jnp.concatenate([own[0, j], own[1, j], other[0, j], other[1, j]], axis=0)
        product = jnp.dot(weights[j], rows, preferred_element_type=jnp.float32)
        product = product.astype(kept.dtype)
        kept[j] = product[:rank]
        sent[j] = product[rank:]


def level_two_apart(weights, own, other, after):
    blocks, rank, size = own.shape
    half = blocks // 2
    part = half // 2
    pair = pl.BlockSpec((2, part, rank, size), lambda i: (0, i, 0, 0))
    return ordered_call(
        level_two_apart_kernel,
        [weights, own.reshape(2, half, rank, size), other.reshape(2, half, rank, size)],
        [pl.BlockSpec((part, 2 * rank, 4 * rank), lambda i: (i, 0, 0)), pair, pair],
        after,
        grid=(2,),
        out_specs=[pl.BlockSpec((part, rank, size), lambda i: (i, 0, 0))] * 2,
        out_shape=[jax.ShapeDtypeStruct((half, rank, size), jnp.bfloat16)] * 2,
        cost_estimate=cost(0, 0),
        name="apart",
    )


def pack_kernel(*refs):
    for i, ref in enumerate(refs[:4]):
        refs[4][:, i] = ref[...]


def pack_chunk(pieces, after):
    half, rank, size = pieces[0].shape
    part = half // 2
    return ordered_call(
        pack_kernel,
        pieces,
        [pl.BlockSpec((part, rank, size), lambda i: (i, 0, 0))] * 4,
        after,
        grid=(2,),
        out_specs=pl.BlockSpec((part, 4, rank, size), lambda i: (i, 0, 0, 0)),
        out_shape=jax.ShapeDtypeStruct((half, 4, rank, size), jnp.bfloat16),
        cost_estimate=cost(0, 0),
        name="pack",
    )


def split_kernel(both, kept, sent):
    kept[...] = both[:, 0]
    sent[...] = both[:, 1]


def split_chunk(both, after):
    half, _, rank, size = both.shape
    part = half // 2
    out = jax.ShapeDtypeStruct((half, rank, size), jnp.bfloat16)
    out_spec = pl.BlockSpec((part, rank, size), lambda i: (i, 0, 0))
    return ordered_call(
        split_kernel,
        [both],
        [pl.BlockSpec((part, 2, rank, size), lambda i: (i, 0, 0, 0))],
        after,
        grid=(2,),
        out_specs=[out_spec, out_spec],
        out_shape=[out, out],
        cost_estimate=cost(0, 8 * half * rank * size),
        name="split",
    )


def compose_kernel(flags, weights, middle, partner, out):
    groups, rank = out.shape[0], weights.shape[1]

    def for_place(low_s, upper_t):
        for j in range(groups):
            rows = jnp.concatenate([weights[j], weights[j + groups]], axis=0)
            for slot in range(4):
                e, f = low_s ^ (slot & 1), upper_t ^ (slot >> 1)
                centre = (partner if slot & 1 else middle)[j + groups * f]
                at = (2 * e + f) * rank
                product = jnp.dot(
                    rows[:, at : at + rank], centre, preferred_element_type=jnp.float32
                )
                out[j, :, slot * rank : (slot + 1) * rank] = product.astype(out.dtype)

    for low_s in range(2):
        for upper_t in range(2):
            here = (flags[2] == low_s) & (flags[1] == upper_t)
            pl.when(here)(functools.partial(for_place, low_s, upper_t))


def composed_three(flags, weights, middle, partner, after):
    blocks, rank, depth = weights.shape
    return ordered_call(
        compose_kernel,
        [flags, weights, middle, partner],
        [pl.BlockSpec(memory_space=pltpu.SMEM)]
        + [pl.BlockSpec(memory_space=pltpu.VMEM)] * 3,
        after,
        out_specs=pl.BlockSpec(memory_space=pltpu.VMEM),
        out_shape=jax.ShapeDtypeStruct((blocks // 2, 2 * rank, depth), jnp.bfloat16),
        cost_estimate=cost(2 * blocks * rank * depth * rank, 6 * blocks * rank * depth),
        name="compose",
    )


def level_three_kernel(count, weights, *refs):
    pieces, out, token = refs[:count], refs[-2], refs[-1]
    token[...] = jnp.zeros_like(token)
    rank = out.shape[2]
    for j in range(out.shape[1]):
        if len(pieces) == 1:
            rows = pieces[0][j].reshape(4 * rank, -1)
        else:
            rows = jnp.concatenate([piece[j] for piece in pieces], axis=0)
        product = jnp.dot(weights[j], rows, preferred_element_type=jnp.float32)
        product = product.astype(out.dtype)
        out[0, j] = product[:rank]
        out[1, j] = product[rank:]


def level_three_chunk(weights, pieces, result, shape, start, after):
    half, rank, size = pieces[0].shape[0], *pieces[0].shape[-2:]
    part = half // 2
    column = start // size
    in_specs = [pl.BlockSpec((part, 2 * rank, 4 * rank), lambda i: (i, 0, 0))]
    if len(pieces) == 1:
        in_specs.append(pl.BlockSpec((part, 4, rank, size), lambda i: (i, 0, 0, 0)))
    else:
        in_specs += [pl.BlockSpec((part, rank, size), lambda i: (i, 0, 0))] * 4
    operands, aliases = [weights, *pieces], {}
    if result is not None:
        in_specs.append(pl.BlockSpec(memory_space=pltpu.HBM))
        operands.append(result)
        aliases = {len(operands) - 1: 0}
    return ordered_call(
        functools.partial(level_three_kernel, len(pieces)),
        operands,
        in_specs,
        after,
        aliases,
        grid=(2,),
        out_specs=[
            pl.BlockSpec((2, part, rank, size), lambda i: (0, i, 0, column)),
            pl.BlockSpec((8, 128), lambda i: (0, 0)),
        ],
        out_shape=[
            jax.ShapeDtypeStruct((2, half, rank, shape[2]), jnp.bfloat16),
            jax.ShapeDtypeStruct((8, 128), jnp.float32),
        ],
        cost_estimate=cost(4 * half * rank * 4 * rank * size, 12 * half * rank * size),
        name="three",
    )


def shards(gathers, level_one, level_two, middle, level_three):
    n_tr, n_pt = lax.axis_size("tr"), lax.axis_size("pt")
    t, s = lax.axis_index("tr"), lax.axis_index("pt")
    flags = jnp.stack([s >> 2, t >> 4, s & 1]).astype(jnp.int32)
    count = len(CHUNKS)
    own, other, both, pieces = {}, {}, {}, {}
    result, last = None, ()

    def one(cs):
        nonlocal last
        outs = level_one_chunks(level_one, gathers, [CHUNKS[c] for c in cs], last)
        last = (outs[0],)
        for c, out in zip(cs, outs):
            own[c] = out
            other[c] = exchanged(out, 0, n_pt // 2)

    def two(c):
        nonlocal last
        if c >= count:
            return
        mixed = level_two_chunk(weights_two, own[c], other[c], last)
        last = (mixed,)
        both[c] = spread(mixed)

    def swapped(kept, sent):
        return (
            kept,
            exchanged(kept, 0, 1),
            exchanged(sent, n_tr // 2, 0),
            exchanged(sent, n_tr // 2, 1),
        )

    def apart(c):
        nonlocal last
        kept, sent = level_two_apart(weights_two, own[c], other[c], last)
        last = (sent,)
        pieces[c] = swapped(kept, sent)

    def pack(c):
        nonlocal last
        packed = pack_chunk(pieces[c], last)
        last = (packed,)
        pieces[c] = (spread(packed),)

    def split(c):
        nonlocal last
        kept, sent = split_chunk(both[c], last)
        last = (sent,)
        pieces[c] = swapped(kept, sent)

    def three(c):
        nonlocal result, last
        if c < 0:
            return
        result, token = level_three_chunk(
            weights_three, pieces[c], result, gathers.shape, CHUNKS[c][0], last
        )
        last = (token,)

    partner = exchanged(middle, 0, 1)
    one([0])
    one([1, 2, 3])
    weights_two = ordered_two(flags, level_two, last)
    last = (weights_two,)
    two(0)
    weights_three = composed_three(flags, level_three, middle, partner, last)
    last = (weights_three,)
    two(1)
    split(0)
    two(2)
    one([4])
    split(1)
    two(3)
    three(0)
    apart(4)
    split(2)
    three(1)
    pack(4)
    split(3)
    three(2)
    three(4)
    three(3)
    return result.reshape(gathers.shape)


def solution(mesh):
    spec = P(("tr", "pt"), None, None)
    return jax.shard_map(
        shards, mesh=mesh, in_specs=(spec,) * 5, out_specs=spec, check_vma=False
    )
```
